32 devices in a mesh: dp: 2 (over core), context: 16 (over z, y, x).
Axes of the slice: x: 2, y: 2, z: 4, core: 2. Of those that a mesh axis runs over, the one named last changes fastest.
Arguments:
- queries: bfloat16 [2, 2048, 4096], P('dp', 'context'), may hold values from -5 to 5
- keys: bfloat16 [2, 2048, 1024], P('dp', 'context'), may hold values from -5 to 5
- values: bfloat16 [2, 2048, 1024], P('dp', 'context'), may hold values from -5 to 5
- d_proj: bfloat16 [2, 2048, 2048], P('dp', 'context'), may hold values from -5 to 5
- out_weight: bfloat16 [4096, 2048], P('context'), may hold values from -0.09375 to 0.09375
- random_blocks: int32 [32, 15], replicated, may hold values from 1 to 15, as said below
Outputs:
- attn_out: bfloat16 [2, 2048, 4096], P('dp', 'context')
- d_queries: bfloat16 [2, 2048, 4096], P('dp', 'context')
- d_keys: bfloat16 [2, 2048, 1024], P('dp', 'context')
- d_values: bfloat16 [2, 2048, 1024], P('dp', 'context')
- d_out_weight: float32 [4096, 2048], P('context')
The draws below stay inside these ranges and needn't reach their ends.
Inputs may be any that keep to these rules, and one draw needn't show every extreme that they name: random_blocks[h, i - 1] is the random key block of query block i of head h; it is never i - 1, i or i + 1.
All inputs are finite; a program needn't handle non-finite values.
Results may differ from the reference program's by a relative error of at most 0.03.
Values may be sent and summed in bfloat16 or wider, within the bound.
A program may use at most 192 MiB of HBM per device.

```python
import jax
import jax.numpy as jnp
from jax import lax

H = 32
KVH = 8
DH = 128
D = 2048
BLOCK = 128
SEQS = 2
SEQ = 2048
HD = 4096


def draw_queries(key, part):
    return jnp.clip(jax.random.normal(jax.random.fold_in(key, 1), (SEQS, SEQ, H * DH), jnp.float32), -5.0, 5.0).astype(jnp.bfloat16)


def draw_keys(key, part):
    return jnp.clip(jax.random.normal(jax.random.fold_in(key, 2), (SEQS, SEQ, KVH * DH), jnp.float32), -5.0, 5.0).astype(jnp.bfloat16)


def draw_random_blocks(key, part):
    block_count = SEQ // BLOCK
    offsets = jax.random.randint(jax.random.fold_in(key, 21), (H, block_count - 1), 0, block_count - 4)
    rows_here = jnp.arange(1, block_count)[None, :]
    lowest = jnp.maximum(rows_here - 1, 1)
    skipped = jnp.where((rows_here >= 2) & (rows_here <= block_count - 2), 3, 2)
    picked = 1 + offsets
    return jnp.where(picked >= lowest, picked + skipped, picked).astype(jnp.int32)


def shard_levels(key, shape, pieces, least, largest):
    loudness, own = 1.0, jax.random.fold_in(key, 6)
    for dim, shards_of in pieces:
        heights = jnp.exp(jax.random.uniform(jax.random.fold_in(own, dim), (shards_of,), jnp.float32, least / len(pieces), largest / len(pieces)))
        loudness = loudness * jnp.repeat(heights, shape[dim] // shards_of).reshape([-1 if axis == dim else 1 for axis in range(len(shape))])
    return loudness


def gaussian(key, shape, scale, most, shards=(), kind=jnp.bfloat16):
    values = jax.random.normal(key, shape, jnp.float32) * scale
    if len(shards) > 0:
        values = shard_levels(key, shape, shards, -0.22, 0.18) * values
    return jnp.clip(values, min=-most, max=most).astype(kind)


def setup_inputs(seed: int = 0) -> dict:
    streams_of = jax.random.split(jax.random.key(seed), 7)
    return {
        "queries": draw_queries(jax.random.fold_in(streams_of[6], 71), 0),
        "keys": draw_keys(jax.random.fold_in(streams_of[6], 71), 0),
        "values": gaussian(streams_of[2], (SEQS, SEQ, KVH * DH), 1.0, 5.0, ((0, 2), (1, 16))),
        "d_proj": gaussian(streams_of[3], (SEQS, SEQ, D), 1.0, 5.0, ((0, 2), (1, 16))),
        "out_weight": gaussian(streams_of[4], (HD, D), HD ** -0.5, 0.09375, ((0, 16),)),
        "random_blocks": draw_random_blocks(jax.random.fold_in(streams_of[6], 71), 0),
    }


def rounded(array):
    return lax.optimization_barrier(array.astype(jnp.bfloat16)).astype(jnp.float32)


def product(form, left_op, right_op):
    return jnp.einsum(form, left_op, right_op, precision=lax.Precision.HIGHEST)


def usable_blocks(block_count):
    positions = jnp.arange(1, block_count)
    always = positions >= 1
    return jnp.stack([always, positions >= 2, always, positions <= block_count - 2, always], axis=1)


def gathered(blocks, chosen):
    block_count = blocks.shape[0]
    global_part = jnp.broadcast_to(blocks[0], (block_count - 1,) + blocks.shape[1:])
    right_part = jnp.concatenate([blocks[2:], jnp.zeros_like(blocks[:1])], axis=0)
    return jnp.stack([global_part, blocks[:-1], blocks[1:], right_part, blocks[chosen]], axis=1)


def returned(parts, chosen, block_count):
    total = jnp.zeros((block_count,) + parts.shape[2:], parts.dtype)
    total = total.at[0].add(jnp.sum(parts[:, 0], axis=0))
    total = total.at[:-1].add(parts[:, 1])
    total = total.at[1:].add(parts[:, 2])
    total = total.at[2:].add(parts[:-1, 3])
    total = total.at[chosen].add(parts[:, 4])
    return total


def one_head(query, key_head, value_head, grad_out, chosen):
    length, head_dim = query.shape
    block_count = length // BLOCK
    scaling = head_dim ** -0.5
    query_f = query.astype(jnp.float32)
    key_f = key_head.astype(jnp.float32)
    value_f = value_head.astype(jnp.float32)
    query_blocks = query_f.reshape(block_count, BLOCK, head_dim)
    key_blocks = key_f.reshape(block_count, BLOCK, head_dim)
    value_blocks = value_f.reshape(block_count, BLOCK, head_dim)
    top_scores = product("bd,ld->bl", query_blocks[0], key_f) * scaling
    top_max = jnp.max(top_scores, axis=1, keepdims=True)
    top_lse = top_max + jnp.log(jnp.sum(jnp.exp(top_scores - top_max), axis=1, keepdims=True))
    top_prob = jnp.exp(top_scores - top_lse)
    top_prob_b = rounded(top_prob)
    top_out = rounded(product("bl,ld->bd", top_prob_b, value_f))
    key_sets = gathered(key_blocks, chosen)
    value_sets = gathered(value_blocks, chosen)
    usable = usable_blocks(block_count)[:, None, :, None]
    scores = product("ibd,ijcd->ibjc", query_blocks[1:], key_sets) * scaling
    masked = jnp.where(usable, scores, -jnp.inf)
    row_max = jnp.max(masked, axis=(2, 3), keepdims=True)
    row_lse = row_max + jnp.log(jnp.sum(jnp.exp(masked - row_max), axis=(2, 3), keepdims=True))
    probs = jnp.exp(masked - row_lse)
    probs_b = rounded(probs)
    rest_out = rounded(product("ibjc,ijcd->ibd", probs_b, value_sets))
    output = jnp.concatenate([top_out[None], rest_out], axis=0).reshape(length, head_dim)
    grad_f = grad_out.astype(jnp.float32)
    row_dot = jnp.sum(grad_f * output, axis=1).reshape(block_count, BLOCK)
    grad_blocks = grad_f.reshape(block_count, BLOCK, head_dim)
    top_dprob = product("bd,ld->bl", grad_blocks[0], value_f)
    top_dscore = rounded(top_prob * (top_dprob - row_dot[0][:, None]))
    top_dquery = product("bl,ld->bd", top_dscore, key_f) * scaling
    key_grad = product("bl,bd->ld", top_dscore, query_blocks[0]) * scaling
    value_grad = product("bl,bd->ld", top_prob_b, grad_blocks[0])
    dprob = product("ibd,ijcd->ibjc", grad_blocks[1:], value_sets)
    dscore = rounded(probs * (dprob - row_dot[1:, :, None, None]))
    rest_dquery = product("ibjc,ijcd->ibd", dscore, key_sets) * scaling
    key_parts = product("ibjc,ibd->ijcd", dscore, query_blocks[1:]) * scaling
    value_parts = product("ibjc,ibd->ijcd", probs_b, grad_blocks[1:])
    key_grad = key_grad + returned(key_parts, chosen, block_count).reshape(length, head_dim)
    value_grad = value_grad + returned(value_parts, chosen, block_count).reshape(length, head_dim)
    query_grad = jnp.concatenate([top_dquery[None], rest_dquery], axis=0).reshape(length, head_dim)
    return (output.astype(jnp.bfloat16), query_grad.astype(jnp.bfloat16),
            key_grad.astype(jnp.bfloat16), value_grad.astype(jnp.bfloat16))


def reference(queries, keys, values, d_proj, out_weight, random_blocks):
    group = H // KVH

    def one_sequence(weight_sum, items):
        query_seq, key_seq, value_seq, grad_seq = items
        grad_heads = jnp.dot(grad_seq, out_weight.T, preferred_element_type=jnp.float32).astype(jnp.bfloat16)

        def per_head(head):
            start = head * DH
            kv_start = (head // group) * DH
            return one_head(lax.dynamic_slice_in_dim(query_seq, start, DH, 1),
                            lax.dynamic_slice_in_dim(key_seq, kv_start, DH, 1),
                            lax.dynamic_slice_in_dim(value_seq, kv_start, DH, 1),
                            lax.dynamic_slice_in_dim(grad_heads, start, DH, 1),
                            random_blocks[head])

        outputs, query_grads, key_grads, value_grads = lax.map(per_head, jnp.arange(H, dtype=jnp.int32))
        attended = jnp.transpose(outputs, (1, 0, 2)).reshape(SEQ, HD)
        query_seq_grad = jnp.transpose(query_grads, (1, 0, 2)).reshape(SEQ, HD)
        key_sum = jnp.sum(key_grads.astype(jnp.float32).reshape(KVH, group, SEQ, DH), axis=1).astype(jnp.bfloat16)
        value_sum = jnp.sum(value_grads.astype(jnp.float32).reshape(KVH, group, SEQ, DH), axis=1).astype(jnp.bfloat16)
        key_seq_grad = jnp.transpose(key_sum, (1, 0, 2)).reshape(SEQ, KVH * DH)
        value_seq_grad = jnp.transpose(value_sum, (1, 0, 2)).reshape(SEQ, KVH * DH)
        weight_sum = weight_sum + jnp.dot(attended.T, grad_seq, preferred_element_type=jnp.float32)
        return weight_sum, (attended, query_seq_grad, key_seq_grad, value_seq_grad)

    weight_sum, results = lax.scan(one_sequence, jnp.zeros((HD, D), jnp.float32), (queries, keys, values, d_proj))
    return results[0], results[1], results[2], results[3], weight_sum
```

```python
import functools

import jax
import jax.numpy as jnp
from jax import lax
from jax.experimental import pallas as pl
from jax.experimental.pallas import tpu as pltpu
from jax.sharding import PartitionSpec as P

DH = 128
BLOCK = 128
MESH = pl.DeviceIdType.MESH
F32 = jnp.float32
BF16 = jnp.bfloat16


def greet(n, m):
    me = lax.axis_index("context")
    sequence = lax.axis_index("dp")
    barrier = pltpu.get_barrier_semaphore()
    for step in range(1, n):
        pl.semaphore_signal(
            barrier, inc=1, device_id=(sequence, lax.rem(me + step, n)), device_id_type=MESH
        )
    for step in range(1, m):
        pl.semaphore_signal(
            barrier, inc=1, device_id=(lax.rem(sequence + step, m), me), device_id_type=MESH
        )
    pl.semaphore_wait(barrier, n - 1 + m - 1)


def spread(n, local_heads, group, q_ref, k_ref, v_ref, g_ref, qa_ref, ka_ref, va_ref, ga_ref,
           own_sem, a2a_send, a2a_recv, far_send, far_recv, mid_send, mid_recv, last_send, last_recv):
    rows = q_ref.shape[0]
    me = lax.axis_index("context")
    sequence = lax.axis_index("dp")
    planes = n // 4
    plane = me // 4
    place = lax.rem(me, 4)
    other_x = plane * 4 + place + 1 - 2 * lax.rem(place, 2)
    other_y = plane * 4 + lax.rem(place + 2, 4)
    half = g_ref.shape[1] // 2
    width = local_heads * DH
    greet(n, 1)

    def remote(src, dst, send, recv, device):
        return pltpu.make_async_remote_copy(
            src_ref=src, dst_ref=dst, send_sem=send, recv_sem=recv,
            device_id=(sequence, device), device_id_type=MESH,
        )

    def forward(block, low, send, recv, device, src=None):
        cols = pl.ds(low, half)
        source = ga_ref.at[block, :, cols] if src is None else src.at[:, cols]
        return remote(source, ga_ref.at[block, :, cols], send, recv, device)

    def columns(device):
        kv = (device * local_heads) // group
        return (
            pl.ds(pl.multiple_of(device * width, DH), width),
            pl.ds(pl.multiple_of(kv * DH, DH), DH),
        )

    mine = pl.ds(pl.multiple_of(me * rows, rows), rows)
    waits = []
    for step in range(1, planes):
        copy = remote(g_ref, ga_ref.at[me], far_send.at[step], far_recv.at[step],
                      lax.rem(plane + step, planes) * 4 + place)
        copy.start()
        waits.append(copy)

    def pass_on(step, src=None):
        block = lax.rem(plane + planes - step, planes) * 4 + place
        one = forward(block, 0, mid_send.at[0, step], mid_recv.at[0, step], other_x, src)
        two = forward(block, half, mid_send.at[1, step], mid_recv.at[1, step], other_y, src)
        thr = forward(block, 0, last_send.at[0, step], last_recv.at[0, step], other_y, src)
        fou = forward(block, half, last_send.at[1, step], last_recv.at[1, step], other_x, src)
        out = [one, two, thr, fou]
        for copy in out:
            copy.start()
        return out

    mids = [pass_on(0, g_ref)]
    qc, kc = columns(me)
    own = [
        pltpu.make_async_copy(g_ref, ga_ref.at[me], own_sem.at[0]),
        pltpu.make_async_copy(q_ref.at[:, qc], qa_ref.at[mine, :], own_sem.at[1]),
        pltpu.make_async_copy(k_ref.at[:, kc], ka_ref.at[mine, :], own_sem.at[2]),
        pltpu.make_async_copy(v_ref.at[:, kc], va_ref.at[mine, :], own_sem.at[3]),
    ]
    for copy in own:
        copy.start()
    for step in range(1, n):
        device = lax.rem(me + step, n)
        qc, kc = columns(device)
        for kind, (src, dst, cols) in enumerate(
            ((q_ref, qa_ref, qc), (k_ref, ka_ref, kc), (v_ref, va_ref, kc))
        ):
            copy = remote(src.at[:, cols], dst.at[mine, :],
                          a2a_send.at[kind, step], a2a_recv.at[kind, step], device)
            copy.start()
            waits.append(copy)
    for step in range(1, planes):
        waits[step - 1].wait_recv()
        mids.append(pass_on(step))
    for step in range(planes):
        base = lax.rem(plane + planes - step, planes) * 4
        from_x = base + place + 1 - 2 * lax.rem(place, 2)
        from_y = base + lax.rem(place + 2, 4)
        mids[step][0].wait_recv()
        five = forward(from_x, 0, last_send.at[2, step], last_recv.at[2, step], other_y)
        five.start()
        mids[step][1].wait_recv()
        six = forward(from_y, half, last_send.at[3, step], last_recv.at[3, step], other_x)
        six.start()
        mids[step] += [five, six]
    for step in range(planes):
        for which in range(2, 6):
            mids[step][which].wait_recv()
        for copy in mids[step]:
            copy.wait_send()
    for number, copy in enumerate(waits):
        if number >= planes - 1:
            copy.wait_recv()
        copy.wait_send()
    for copy in own:
        copy.wait()


def attend(local_heads, chosen_ref, q_ref, k_ref, v_ref, g_ref, o_ref, dq_ref, dk_ref, dv_ref,
           dk_acc, dv_acc):
    length = q_ref.shape[0]
    blocks = length // BLOCK
    scaling = DH ** (-0.5)
    dk_acc[...] = jnp.zeros_like(dk_acc)
    dv_acc[...] = jnp.zeros_like(dv_acc)

    def nt(a, b):
        return lax.dot_general(a, b, (((1,), (1,)), ((), ())), preferred_element_type=F32)

    def nn(a, b):
        return lax.dot_general(a, b, (((1,), (0,)), ((), ())), preferred_element_type=F32)

    def tn(a, b):
        return lax.dot_general(a, b, (((0,), (0,)), ((), ())), preferred_element_type=F32)

    def at(block):
        return pl.ds(pl.multiple_of(block * BLOCK, BLOCK), BLOCK)

    def stacked(ref, block):
        rows = ref[at(block), :]
        return jnp.concatenate([rows[:, h * DH:(h + 1) * DH] for h in range(local_heads)], axis=0)

    def unstack(ref, block, value):
        ref[at(block), :] = jnp.concatenate(
            [value[h * BLOCK:(h + 1) * BLOCK] for h in range(local_heads)], axis=1
        ).astype(BF16)

    q = stacked(q_ref, 0)
    g = stacked(g_ref, 0)
    s = nt(q, k_ref[...]) * scaling
    e = jnp.exp(s - jnp.max(s, axis=1, keepdims=True))
    p = e * (1.0 / jnp.sum(e, axis=1, keepdims=True))
    pb = p.astype(BF16)
    o = nn(pb, v_ref[...]).astype(BF16)
    unstack(o_ref, 0, o)
    row_dot = jnp.sum(g.astype(F32) * o.astype(F32), axis=1, keepdims=True)
    ds = (p * (nt(g, v_ref[...]) - row_dot)).astype(BF16)
    unstack(dq_ref, 0, nn(ds, k_ref[...]) * scaling)
    dk_acc[...] += tn(ds, q)
    dv_acc[...] += tn(pb, g)

    def body(i, carry):
        right = jnp.minimum(i + 1, blocks - 1)
        near = [0, i - 1, i, right]
        picked = [chosen_ref[h, i - 1] for h in range(local_heads)]
        q = stacked(q_ref, i)
        g = stacked(g_ref, i)
        kn = jnp.concatenate([k_ref[at(b), :] for b in near], axis=0)
        vn = jnp.concatenate([v_ref[at(b), :] for b in near], axis=0)
        kr = [k_ref[at(b), :] for b in picked]
        vr = [v_ref[at(b), :] for b in picked]

        def per_head(op, a, b):
            return jnp.concatenate(
                [op(a[h * BLOCK:(h + 1) * BLOCK], b[h]) for h in range(local_heads)], axis=0
            )

        sn = nt(q, kn) * scaling
        s1 = jnp.where(i >= 2, sn[:, BLOCK:2 * BLOCK], -jnp.inf)
        s3 = jnp.where(i <= blocks - 2, sn[:, 3 * BLOCK:], -jnp.inf)
        s = jnp.concatenate(
            [sn[:, :BLOCK], s1, sn[:, 2 * BLOCK:3 * BLOCK], s3, per_head(nt, q, kr) * scaling], axis=1
        )
        e = jnp.exp(s - jnp.max(s, axis=1, keepdims=True))
        p = e * (1.0 / jnp.sum(e, axis=1, keepdims=True))
        pb = p.astype(BF16)
        pn, pr = pb[:, :4 * BLOCK], pb[:, 4 * BLOCK:]
        o = (nn(pn, vn) + per_head(nn, pr, vr)).astype(BF16)
        unstack(o_ref, i, o)
        row_dot = jnp.sum(g.astype(F32) * o.astype(F32), axis=1, keepdims=True)
        dp = jnp.concatenate([nt(g, vn), per_head(nt, g, vr)], axis=1)
        ds = (p * (dp - row_dot)).astype(BF16)
        dn, dr = ds[:, :4 * BLOCK], ds[:, 4 * BLOCK:]
        unstack(dq_ref, i, (nn(dn, kn) + per_head(nn, dr, kr)) * scaling)
        dkn = tn(dn, q)
        dvn = tn(pn, g)
        for slot, b in enumerate(near):
            dk_acc[at(b), :] += dkn[slot * BLOCK:(slot + 1) * BLOCK]
            dv_acc[at(b), :] += dvn[slot * BLOCK:(slot + 1) * BLOCK]
        for h in range(local_heads):
            rows = slice(h * BLOCK, (h + 1) * BLOCK)
            dk_acc[at(picked[h]), :] += tn(dr[rows], q[rows])
            dv_acc[at(picked[h]), :] += tn(pr[rows], g[rows])
        return carry

    lax.fori_loop(1, blocks, body, 0)
    dk_ref[...] = (dk_acc[...] * scaling).astype(BF16)
    dv_ref[...] = dv_acc[...].astype(BF16)


def bring_back(n, m, kv_heads, o_ref, dq_ref, dk_ref, dv_ref, w_ref, oo_ref, dqo_ref, dko_ref, dvo_ref,
               dw_ref, k_parts, v_parts, w_parts, own_sem, send, recv, w_send, w_recv):
    rows = oo_ref.shape[0]
    width = o_ref.shape[1]
    me = lax.axis_index("context")
    sequence = lax.axis_index("dp")
    greet(n, m)
    cols = pl.ds(pl.multiple_of(me * width, DH), width)
    w_copies = []
    for step in range(1, m):
        copy = pltpu.make_async_remote_copy(
            src_ref=w_ref, dst_ref=w_parts.at[sequence], send_sem=w_send.at[step],
            recv_sem=w_recv.at[step], device_id=(lax.rem(sequence + step, m), me), device_id_type=MESH,
        )
        copy.start()
        w_copies.append(copy)
    pairs = (
        (o_ref, oo_ref.at[:, cols]),
        (dq_ref, dqo_ref.at[:, cols]),
        (dk_ref, k_parts.at[me]),
        (dv_ref, v_parts.at[me]),
    )
    copies = []
    for step in range(1, n):
        device = lax.rem(me + step, n)
        theirs = pl.ds(pl.multiple_of(device * rows, rows), rows)
        for kind, (src, dst) in enumerate(pairs):
            copy = pltpu.make_async_remote_copy(
                src_ref=src.at[theirs, :], dst_ref=dst, send_sem=send.at[kind, step],
                recv_sem=recv.at[kind, step], device_id=(sequence, device), device_id_type=MESH,
            )
            copy.start()
            copies.append(copy)
    mine = pl.ds(pl.multiple_of(me * rows, rows), rows)
    own = [
        pltpu.make_async_copy(src.at[mine, :], dst, own_sem.at[kind])
        for kind, (src, dst) in enumerate(pairs)
    ]
    own.append(pltpu.make_async_copy(w_ref, w_parts.at[sequence], own_sem.at[4]))
    for copy in own:
        copy.start()
    own[4].wait()
    for copy in w_copies:
        copy.wait()
    tile = 32

    @pl.loop(0, w_ref.shape[0] // tile)
    def _(t):
        at = pl.ds(pl.multiple_of(t * tile, tile), tile)
        total = w_parts[0, at, :].astype(F32)
        for other in range(1, m):
            total = total + w_parts[other, at, :].astype(F32)
        dw_ref[at, :] = total

    for copy in own[:4]:
        copy.wait()
    for copy in copies:
        copy.wait()
    per = n // kv_heads
    for parts, out in ((k_parts, dko_ref), (v_parts, dvo_ref)):
        for kv in range(kv_heads):
            total = parts[kv * per].astype(F32)
            for other in range(1, per):
                total = total + parts[kv * per + other].astype(F32)
            out[:, kv * DH:(kv + 1) * DH] = total.astype(BF16)


def local(queries, keys, values, d_proj, out_weight, random_blocks):
    n = lax.axis_size("context")
    m = lax.axis_size("dp")
    rows = queries.shape[1]
    heads = queries.shape[2] // DH
    kv_heads = keys.shape[2] // DH
    group = heads // kv_heads
    local_heads = heads // n
    width = local_heads * DH
    columns = d_proj.shape[2]
    length = rows * n
    planes = n // 4
    anywhere = pl.BlockSpec(memory_space=pl.ANY)
    vmem = pl.BlockSpec(memory_space=pltpu.VMEM)
    shape = jax.ShapeDtypeStruct
    dma = pltpu.SemaphoreType.DMA

    q_all, k_all, v_all, g_all = pl.pallas_call(
        functools.partial(spread, n, local_heads, group),
        out_shape=(
            shape((length, width), BF16),
            shape((length, DH), BF16),
            shape((length, DH), BF16),
            shape((n, rows, columns), BF16),
        ),
        in_specs=[anywhere] * 4,
        out_specs=(anywhere,) * 4,
        scratch_shapes=[
            dma((4,)),
            dma((3, n)), dma((3, n)),
            dma((planes,)), dma((planes,)),
            dma((2, planes)), dma((2, planes)),
            dma((4, planes)), dma((4, planes)),
        ],
        compiler_params=pltpu.CompilerParams(collective_id=0, has_side_effects=True),
        name="spread",
    )(queries[0], keys[0], values[0], d_proj[0])

    grad_rows = g_all.reshape(length, columns)
    grad_out = lax.dot_general(
        grad_rows, out_weight, (((1,), (1,)), ((), ())), preferred_element_type=F32
    ).astype(BF16)
    chosen = lax.dynamic_slice_in_dim(
        random_blocks, lax.axis_index("context") * local_heads, local_heads, 0
    )
    out, dq, dk, dv = pl.pallas_call(
        functools.partial(attend, local_heads),
        out_shape=(
            shape((length, width), BF16),
            shape((length, width), BF16),
            shape((length, DH), BF16),
            shape((length, DH), BF16),
        ),
        in_specs=[pl.BlockSpec(memory_space=pltpu.SMEM)] + [vmem] * 4,
        out_specs=(vmem,) * 4,
        scratch_shapes=[pltpu.VMEM((length, DH), F32), pltpu.VMEM((length, DH), F32)],
        compiler_params=pltpu.CompilerParams(vmem_limit_bytes=48 * 1024 * 1024),
        name="attend",
    )(chosen, q_all, k_all, v_all, grad_out)
    weight_part = lax.dot_general(
        out, grad_rows, (((0,), (0,)), ((), ())), preferred_element_type=F32
    ).astype(BF16)
    attended, d_queries, d_keys, d_values, d_weight = pl.pallas_call(
        functools.partial(bring_back, n, m, kv_heads),
        out_shape=(
            shape((rows, heads * DH), BF16),
            shape((rows, heads * DH), BF16),
            shape((rows, kv_heads * DH), BF16),
            shape((rows, kv_heads * DH), BF16),
            shape((width, columns), F32),
        ),
        in_specs=[anywhere] * 5,
        out_specs=(anywhere, anywhere, vmem, vmem, vmem),
        scratch_shapes=[
            pltpu.VMEM((n, rows, DH), BF16),
            pltpu.VMEM((n, rows, DH), BF16),
            pltpu.VMEM((m, width, columns), BF16),
            dma((5,)),
            dma((4, n)), dma((4, n)),
            dma((m,)), dma((m,)),
        ],
        compiler_params=pltpu.CompilerParams(
            collective_id=1, has_side_effects=True, vmem_limit_bytes=48 * 1024 * 1024
        ),
        name="bring_back",
    )(out, dq, dk, dv, weight_part)
    return (attended[None], d_queries[None], d_keys[None], d_values[None], d_weight)


def solution(mesh):
    in_specs = (
        P("dp", "context", None),
        P("dp", "context", None),
        P("dp", "context", None),
        P("dp", "context", None),
        P("context", None),
        P(),
    )
    out_specs = (
        P("dp", "context", None),
        P("dp", "context", None),
        P("dp", "context", None),
        P("dp", "context", None),
        P("context", None),
    )
    return jax.shard_map(local, mesh=mesh, in_specs=in_specs, out_specs=out_specs, check_vma=False)
```

```python
import functools

import jax
import jax.numpy as jnp
from jax import lax
from jax.experimental import pallas as pl
from jax.experimental.pallas import tpu as pltpu
from jax.sharding import PartitionSpec as P

DH = 128
BLOCK = 128
MESH = pl.DeviceIdType.MESH
F32 = jnp.float32
BF16 = jnp.bfloat16


def greet(n, m):
    me = lax.axis_index("context")
    sequence = lax.axis_index("dp")
    barrier = pltpu.get_barrier_semaphore()
    for step in range(1, n):
        pl.semaphore_signal(
            barrier, inc=1, device_id=(sequence, lax.rem(me + step, n)), device_id_type=MESH
        )
    for step in range(1, m):
        pl.semaphore_signal(
            barrier, inc=1, device_id=(lax.rem(sequence + step, m), me), device_id_type=MESH
        )
    pl.semaphore_wait(barrier, n - 1 + m - 1)


def spread(n, local_heads, group, q_ref, k_ref, v_ref, g_ref, w_ref, qa_ref, ka_ref, va_ref, ga_ref,
           grad_ref, tiles, own_sem, tile_sem, a2a_send, a2a_recv, far_send, far_recv, mid_send, mid_recv, last_send, last_recv):
    rows = q_ref.shape[0]
    me = lax.axis_index("context")
    sequence = lax.axis_index("dp")
    planes = n // 4
    plane = me // 4
    place = lax.rem(me, 4)
    other_x = plane * 4 + place + 1 - 2 * lax.rem(place, 2)
    other_y = plane * 4 + lax.rem(place + 2, 4)
    half = g_ref.shape[1] // 2
    width = local_heads * DH
    greet(n, 1)

    def remote(src, dst, send, recv, device):
        return pltpu.make_async_remote_copy(
            src_ref=src, dst_ref=dst, send_sem=send, recv_sem=recv,
            device_id=(sequence, device), device_id_type=MESH,
        )

    def forward(block, low, send, recv, device, src=None):
        cols = pl.ds(low, half)
        source = ga_ref.at[block, :, cols] if src is None else src.at[:, cols]
        return remote(source, ga_ref.at[block, :, cols], send, recv, device)

    def columns(device):
        kv = (device * local_heads) // group
        return (
            pl.ds(pl.multiple_of(device * width, DH), width),
            pl.ds(pl.multiple_of(kv * DH, DH), DH),
        )

    mine = pl.ds(pl.multiple_of(me * rows, rows), rows)
    waits = []
    for step in range(1, planes):
        copy = remote(g_ref, ga_ref.at[me], far_send.at[step], far_recv.at[step],
                      lax.rem(plane + step, planes) * 4 + place)
        copy.start()
        waits.append(copy)

    def pass_on(step, src=None):
        block = lax.rem(plane + planes - step, planes) * 4 + place
        one = forward(block, 0, mid_send.at[0, step], mid_recv.at[0, step], other_x, src)
        two = forward(block, half, mid_send.at[1, step], mid_recv.at[1, step], other_y, src)
        thr = forward(block, 0, last_send.at[0, step], last_recv.at[0, step], other_y, src)
        fou = forward(block, half, last_send.at[1, step], last_recv.at[1, step], other_x, src)
        out = [one, two, thr, fou]
        for copy in out:
            copy.start()
        return out

    mids = [pass_on(0, g_ref)]
    qc, kc = columns(me)
    own = [
        pltpu.make_async_copy(g_ref, ga_ref.at[me], own_sem.at[0]),
        pltpu.make_async_copy(q_ref.at[:, qc], qa_ref.at[mine, :], own_sem.at[1]),
        pltpu.make_async_copy(k_ref.at[:, kc], ka_ref.at[mine, :], own_sem.at[2]),
        pltpu.make_async_copy(v_ref.at[:, kc], va_ref.at[mine, :], own_sem.at[3]),
    ]
    for copy in own:
        copy.start()
    for step in range(1, n):
        device = lax.rem(me + step, n)
        qc, kc = columns(device)
        for kind, (src, dst, cols) in enumerate(
            ((q_ref, qa_ref, qc), (k_ref, ka_ref, kc), (v_ref, va_ref, kc))
        ):
            copy = remote(src.at[:, cols], dst.at[mine, :],
                          a2a_send.at[kind, step], a2a_recv.at[kind, step], device)
            copy.start()
            waits.append(copy)
    for step in range(1, planes):
        waits[step - 1].wait_recv()
        mids.append(pass_on(step))
    for step in range(planes):
        base = lax.rem(plane + planes - step, planes) * 4
        from_x = base + place + 1 - 2 * lax.rem(place, 2)
        from_y = base + lax.rem(place + 2, 4)
        mids[step][0].wait_recv()
        five = forward(from_x, 0, last_send.at[2, step], last_recv.at[2, step], other_y)
        five.start()
        mids[step][1].wait_recv()
        six = forward(from_y, half, last_send.at[3, step], last_recv.at[3, step], other_x)
        six.start()
        mids[step] += [five, six]
    own[0].wait()
    for step in range(planes):
        for which in range(2, 6):
            mids[step][which].wait_recv()
        base = lax.rem(plane + planes - step, planes) * 4
        loads = [
            pltpu.make_async_copy(ga_ref.at[base + part], tiles.at[part], tile_sem.at[part])
            for part in range(4)
        ]
        for copy in loads:
            copy.start()
        for copy in loads:
            copy.wait()

        @pl.loop(0, 4)
        def _(part):
            at = pl.ds(pl.multiple_of((base + part) * rows, rows), rows)
            grad_ref[at, :] = lax.dot_general(
                tiles[part], w_ref[...], (((1,), (1,)), ((), ())), preferred_element_type=F32
            ).astype(BF16)

        for copy in mids[step]:
            copy.wait_send()
    for number, copy in enumerate(waits):
        if number >= planes - 1:
            copy.wait_recv()
        copy.wait_send()
    for copy in own[1:]:
        copy.wait()


def attend(local_heads, chosen_ref, q_ref, k_ref, v_ref, g_ref, o_ref, dq_ref, dk_ref, dv_ref,
           dk_acc, dv_acc):
    length = q_ref.shape[0]
    blocks = length // BLOCK
    scaling = DH ** (-0.5)
    dk_acc[...] = jnp.zeros_like(dk_acc)
    dv_acc[...] = jnp.zeros_like(dv_acc)

    def nt(a, b):
        return lax.dot_general(a, b, (((1,), (1,)), ((), ())), preferred_element_type=F32)

    def nn(a, b):
        return lax.dot_general(a, b, (((1,), (0,)), ((), ())), preferred_element_type=F32)

    def tn(a, b):
        return lax.dot_general(a, b, (((0,), (0,)), ((), ())), preferred_element_type=F32)

    def at(block):
        return pl.ds(pl.multiple_of(block * BLOCK, BLOCK), BLOCK)

    def stacked(ref, block):
        rows = ref[at(block), :]
        return jnp.concatenate([rows[:, h * DH:(h + 1) * DH] for h in range(local_heads)], axis=0)

    def unstack(ref, block, value):
        ref[at(block), :] = jnp.concatenate(
            [value[h * BLOCK:(h + 1) * BLOCK] for h in range(local_heads)], axis=1
        ).astype(BF16)

    q = stacked(q_ref, 0)
    g = stacked(g_ref, 0)
    s = nt(q, k_ref[...]) * scaling
    e = jnp.exp(s - jnp.max(s, axis=1, keepdims=True))
    p = e * (1.0 / jnp.sum(e, axis=1, keepdims=True))
    pb = p.astype(BF16)
    o = nn(pb, v_ref[...]).astype(BF16)
    unstack(o_ref, 0, o)
    row_dot = jnp.sum(g.astype(F32) * o.astype(F32), axis=1, keepdims=True)
    ds = (p * (nt(g, v_ref[...]) - row_dot)).astype(BF16)
    unstack(dq_ref, 0, nn(ds, k_ref[...]) * scaling)
    dk_acc[...] += tn(ds, q)
    dv_acc[...] += tn(pb, g)

    def body(i, carry):
        right = jnp.minimum(i + 1, blocks - 1)
        near = [0, i - 1, i, right]
        picked = [chosen_ref[h, i - 1] for h in range(local_heads)]
        q = stacked(q_ref, i)
        g = stacked(g_ref, i)
        kn = jnp.concatenate([k_ref[at(b), :] for b in near], axis=0)
        vn = jnp.concatenate([v_ref[at(b), :] for b in near], axis=0)
        kr = [k_ref[at(b), :] for b in picked]
        vr = [v_ref[at(b), :] for b in picked]

        def per_head(op, a, b):
            return jnp.concatenate(
                [op(a[h * BLOCK:(h + 1) * BLOCK], b[h]) for h in range(local_heads)], axis=0
            )

        sn = nt(q, kn) * scaling
        s1 = jnp.where(i >= 2, sn[:, BLOCK:2 * BLOCK], -jnp.inf)
        s3 = jnp.where(i <= blocks - 2, sn[:, 3 * BLOCK:], -jnp.inf)
        s = jnp.concatenate(
            [sn[:, :BLOCK], s1, sn[:, 2 * BLOCK:3 * BLOCK], s3, per_head(nt, q, kr) * scaling], axis=1
        )
        e = jnp.exp(s - jnp.max(s, axis=1, keepdims=True))
        p = e * (1.0 / jnp.sum(e, axis=1, keepdims=True))
        pb = p.astype(BF16)
        pn, pr = pb[:, :4 * BLOCK], pb[:, 4 * BLOCK:]
        o = (nn(pn, vn) + per_head(nn, pr, vr)).astype(BF16)
        unstack(o_ref, i, o)
        row_dot = jnp.sum(g.astype(F32) * o.astype(F32), axis=1, keepdims=True)
        dp = jnp.concatenate([nt(g, vn), per_head(nt, g, vr)], axis=1)
        ds = (p * (dp - row_dot)).astype(BF16)
        dn, dr = ds[:, :4 * BLOCK], ds[:, 4 * BLOCK:]
        unstack(dq_ref, i, (nn(dn, kn) + per_head(nn, dr, kr)) * scaling)
        dkn = tn(dn, q)
        dvn = tn(pn, g)
        for slot, b in enumerate(near):
            dk_acc[at(b), :] += dkn[slot * BLOCK:(slot + 1) * BLOCK]
            dv_acc[at(b), :] += dvn[slot * BLOCK:(slot + 1) * BLOCK]
        for h in range(local_heads):
            rows = slice(h * BLOCK, (h + 1) * BLOCK)
            dk_acc[at(picked[h]), :] += tn(dr[rows], q[rows])
            dv_acc[at(picked[h]), :] += tn(pr[rows], g[rows])
        return carry

    lax.fori_loop(1, blocks, body, 0)
    dk_ref[...] = (dk_acc[...] * scaling).astype(BF16)
    dv_ref[...] = dv_acc[...].astype(BF16)


def bring_back(n, m, kv_heads, o_ref, dq_ref, dk_ref, dv_ref, g_ref, oo_ref, dqo_ref, dko_ref, dvo_ref,
               dw_ref, k_parts, v_parts, w_own, w_parts, o_vmem, o_turned, g_vmem, own_sem, send, recv, w_send, w_recv):
    rows = oo_ref.shape[0]
    width = o_ref.shape[1]
    me = lax.axis_index("context")
    sequence = lax.axis_index("dp")
    greet(n, m)
    cols = pl.ds(pl.multiple_of(me * width, DH), width)
    pairs = (
        (o_ref, oo_ref.at[:, cols]),
        (dq_ref, dqo_ref.at[:, cols]),
        (dk_ref, k_parts.at[me]),
        (dv_ref, v_parts.at[me]),
    )
    copies = []

    def send_out(kinds):
        for step in range(1, n):
            device = lax.rem(me + step, n)
            theirs = pl.ds(pl.multiple_of(device * rows, rows), rows)
            for kind in kinds:
                src, dst = pairs[kind]
                copy = pltpu.make_async_remote_copy(
                    src_ref=src.at[theirs, :], dst_ref=dst, send_sem=send.at[kind, step],
                    recv_sem=recv.at[kind, step], device_id=(sequence, device), device_id_type=MESH,
                )
                copy.start()
                copies.append(copy)

    load_o = pltpu.make_async_copy(o_ref, o_vmem, own_sem.at[4])
    load_g = pltpu.make_async_copy(g_ref, g_vmem, own_sem.at[5])
    load_o.start()
    load_g.start()
    send_out((0,))
    mine = pl.ds(pl.multiple_of(me * rows, rows), rows)
    own = [
        pltpu.make_async_copy(src.at[mine, :], dst, own_sem.at[kind])
        for kind, (src, dst) in enumerate(pairs)
    ]
    load_o.wait()

    @pl.loop(0, n)
    def _(t):
        at = pl.ds(pl.multiple_of(t * rows, rows), rows)
        o_turned[:, at] = o_vmem[at, :].T

    load_g.wait()
    wide = 256

    @pl.loop(0, g_ref.shape[1] // wide)
    def _(t):
        at = pl.ds(pl.multiple_of(t * wide, wide), wide)
        w_own[:, at] = lax.dot_general(
            o_turned[...], g_vmem[:, at], (((1,), (0,)), ((), ())), preferred_element_type=F32
        ).astype(BF16)

    w_copies = []
    for step in range(1, m):
        copy = pltpu.make_async_remote_copy(
            src_ref=w_own, dst_ref=w_parts.at[sequence], send_sem=w_send.at[step],
            recv_sem=w_recv.at[step], device_id=(lax.rem(sequence + step, m), me), device_id_type=MESH,
        )
        copy.start()
        w_copies.append(copy)
    send_out((1, 2, 3))
    for copy in own:
        copy.start()
    to_slot = pltpu.make_async_copy(w_own, w_parts.at[sequence], own_sem.at[6])
    to_slot.start()
    to_slot.wait()
    for copy in w_copies:
        copy.wait()
    tile = 32

    @pl.loop(0, w_own.shape[0] // tile)
    def _(t):
        at = pl.ds(pl.multiple_of(t * tile, tile), tile)
        total = w_parts[0, at, :].astype(F32)
        for other in range(1, m):
            total = total + w_parts[other, at, :].astype(F32)
        dw_ref[at, :] = total

    for copy in own[:4]:
        copy.wait()
    for copy in copies:
        copy.wait()
    per = n // kv_heads
    for parts, out in ((k_parts, dko_ref), (v_parts, dvo_ref)):
        for kv in range(kv_heads):
            total = parts[kv * per].astype(F32)
            for other in range(1, per):
                total = total + parts[kv * per + other].astype(F32)
            out[:, kv * DH:(kv + 1) * DH] = total.astype(BF16)


def local(queries, keys, values, d_proj, out_weight, random_blocks):
    n = lax.axis_size("context")
    m = lax.axis_size("dp")
    rows = queries.shape[1]
    heads = queries.shape[2] // DH
    kv_heads = keys.shape[2] // DH
    group = heads // kv_heads
    local_heads = heads // n
    width = local_heads * DH
    columns = d_proj.shape[2]
    length = rows * n
    planes = n // 4
    anywhere = pl.BlockSpec(memory_space=pl.ANY)
    vmem = pl.BlockSpec(memory_space=pltpu.VMEM)
    shape = jax.ShapeDtypeStruct
    dma = pltpu.SemaphoreType.DMA

    q_all, k_all, v_all, g_all, grad_out = pl.pallas_call(
        functools.partial(spread, n, local_heads, group),
        out_shape=(
            shape((length, width), BF16),
            shape((length, DH), BF16),
            shape((length, DH), BF16),
            shape((n, rows, columns), BF16),
            shape((length, width), BF16),
        ),
        in_specs=[anywhere] * 4 + [vmem],
        out_specs=(anywhere,) * 4 + (vmem,),
        scratch_shapes=[
            pltpu.VMEM((4, rows, columns), BF16),
            dma((4,)),
            dma((4,)),
            dma((3, n)), dma((3, n)),
            dma((planes,)), dma((planes,)),
            dma((2, planes)), dma((2, planes)),
            dma((4, planes)), dma((4, planes)),
        ],
        compiler_params=pltpu.CompilerParams(
            collective_id=0, has_side_effects=True, vmem_limit_bytes=56 * 1024 * 1024
        ),
        name="spread",
    )(queries[0], keys[0], values[0], d_proj[0], out_weight)

    chosen = lax.dynamic_slice_in_dim(
        random_blocks, lax.axis_index("context") * local_heads, local_heads, 0
    )
    out, dq, dk, dv = pl.pallas_call(
        functools.partial(attend, local_heads),
        out_shape=(
            shape((length, width), BF16),
            shape((length, width), BF16),
            shape((length, DH), BF16),
            shape((length, DH), BF16),
        ),
        in_specs=[pl.BlockSpec(memory_space=pltpu.SMEM)] + [vmem] * 4,
        out_specs=(vmem,) * 4,
        scratch_shapes=[pltpu.VMEM((length, DH), F32), pltpu.VMEM((length, DH), F32)],
        compiler_params=pltpu.CompilerParams(vmem_limit_bytes=48 * 1024 * 1024),
        name="attend",
    )(chosen, q_all, k_all, v_all, grad_out)
    attended, d_queries, d_keys, d_values, d_weight = pl.pallas_call(
        functools.partial(bring_back, n, m, kv_heads),
        out_shape=(
            shape((rows, heads * DH), BF16),
            shape((rows, heads * DH), BF16),
            shape((rows, kv_heads * DH), BF16),
            shape((rows, kv_heads * DH), BF16),
            shape((width, columns), F32),
        ),
        in_specs=[anywhere] * 5,
        out_specs=(anywhere, anywhere, vmem, vmem, vmem),
        scratch_shapes=[
            pltpu.VMEM((n, rows, DH), BF16),
            pltpu.VMEM((n, rows, DH), BF16),
            pltpu.VMEM((width, columns), BF16),
            pltpu.VMEM((m, width, columns), BF16),
            pltpu.VMEM((length, width), BF16),
            pltpu.VMEM((width, length), BF16),
            pltpu.VMEM((length, columns), BF16),
            dma((7,)),
            dma((4, n)), dma((4, n)),
            dma((m,)), dma((m,)),
        ],
        compiler_params=pltpu.CompilerParams(
            collective_id=1, has_side_effects=True, vmem_limit_bytes=48 * 1024 * 1024
        ),
        name="bring_back",
    )(out, dq, dk, dv, g_all.reshape(length, columns))
    return (attended[None], d_queries[None], d_keys[None], d_values[None], d_weight)


def solution(mesh):
    in_specs = (
        P("dp", "context", None),
        P("dp", "context", None),
        P("dp", "context", None),
        P("dp", "context", None),
        P("context", None),
        P(),
    )
    out_specs = (
        P("dp", "context", None),
        P("dp", "context", None),
        P("dp", "context", None),
        P("dp", "context", None),
        P("context", None),
    )
    return jax.shard_map(local, mesh=mesh, in_specs=in_specs, out_specs=out_specs, check_vma=False)
```

```python
import functools

import jax
import jax.numpy as jnp
from jax import lax
from jax.experimental import pallas as pl
from jax.experimental.pallas import tpu as pltpu
from jax.sharding import PartitionSpec as P

DH = 128
BLOCK = 128
MESH = pl.DeviceIdType.MESH
F32 = jnp.float32
BF16 = jnp.bfloat16


def greet(n, m):
    me = lax.axis_index("context")
    sequence = lax.axis_index("dp")
    barrier = pltpu.get_barrier_semaphore()
    for step in range(1, n):
        pl.semaphore_signal(
            barrier, inc=1, device_id=(sequence, lax.rem(me + step, n)), device_id_type=MESH
        )
    for step in range(1, m):
        pl.semaphore_signal(
            barrier, inc=1, device_id=(lax.rem(sequence + step, m), me), device_id_type=MESH
        )
    pl.semaphore_wait(barrier, n - 1 + m - 1)


def spread(n, local_heads, group, q_ref, k_ref, v_ref, g_ref, w_ref, qa_ref, ka_ref, va_ref, ga_ref,
           grad_ref, tiles, own_sem, tile_sem, a2a_send, a2a_recv, far_send, far_recv, mid_send, mid_recv, last_send, last_recv):
    rows = q_ref.shape[0]
    me = lax.axis_index("context")
    sequence = lax.axis_index("dp")
    planes = n // 4
    plane = me // 4
    place = lax.rem(me, 4)
    other_x = plane * 4 + place + 1 - 2 * lax.rem(place, 2)
    other_y = plane * 4 + lax.rem(place + 2, 4)
    half = g_ref.shape[1] // 2
    width = local_heads * DH
    greet(n, 1)

    def remote(src, dst, send, recv, device):
        return pltpu.make_async_remote_copy(
            src_ref=src, dst_ref=dst, send_sem=send, recv_sem=recv,
            device_id=(sequence, device), device_id_type=MESH,
        )

    def forward(block, low, send, recv, device, src=None):
        cols = pl.ds(low, half)
        source = ga_ref.at[block, :, cols] if src is None else src.at[:, cols]
        return remote(source, ga_ref.at[block, :, cols], send, recv, device)

    def columns(device):
        kv = (device * local_heads) // group
        return (
            pl.ds(pl.multiple_of(device * width, DH), width),
            pl.ds(pl.multiple_of(kv * DH, DH), DH),
        )

    mine = pl.ds(pl.multiple_of(me * rows, rows), rows)
    waits = []
    for step in range(1, planes):
        copy = remote(g_ref, ga_ref.at[me], far_send.at[step], far_recv.at[step],
                      lax.rem(plane + step, planes) * 4 + place)
        copy.start()
        waits.append(copy)

    def pass_on(step, src=None):
        block = lax.rem(plane + planes - step, planes) * 4 + place
        one = forward(block, 0, mid_send.at[0, step], mid_recv.at[0, step], other_x, src)
        two = forward(block, half, mid_send.at[1, step], mid_recv.at[1, step], other_y, src)
        thr = forward(block, 0, last_send.at[0, step], last_recv.at[0, step], other_y, src)
        fou = forward(block, half, last_send.at[1, step], last_recv.at[1, step], other_x, src)
        out = [one, two, thr, fou]
        for copy in out:
            copy.start()
        return out

    mids = [pass_on(0, g_ref)]
    qc, kc = columns(me)
    own = [
        pltpu.make_async_copy(g_ref, ga_ref.at[me], own_sem.at[0]),
        pltpu.make_async_copy(q_ref.at[:, qc], qa_ref.at[mine, :], own_sem.at[1]),
        pltpu.make_async_copy(k_ref.at[:, kc], ka_ref.at[mine, :], own_sem.at[2]),
        pltpu.make_async_copy(v_ref.at[:, kc], va_ref.at[mine, :], own_sem.at[3]),
    ]
    for copy in own:
        copy.start()
    for step in range(1, n):
        device = lax.rem(me + step, n)
        qc, kc = columns(device)
        for kind, (src, dst, cols) in enumerate(
            ((q_ref, qa_ref, qc), (k_ref, ka_ref, kc), (v_ref, va_ref, kc))
        ):
            copy = remote(src.at[:, cols], dst.at[mine, :],
                          a2a_send.at[kind, step], a2a_recv.at[kind, step], device)
            copy.start()
            waits.append(copy)
    for step in range(1, planes):
        waits[step - 1].wait_recv()
        mids.append(pass_on(step))
    for step in range(planes):
        base = lax.rem(plane + planes - step, planes) * 4
        from_x = base + place + 1 - 2 * lax.rem(place, 2)
        from_y = base + lax.rem(place + 2, 4)
        mids[step][0].wait_recv()
        five = forward(from_x, 0, last_send.at[2, step], last_recv.at[2, step], other_y)
        five.start()
        mids[step][1].wait_recv()
        six = forward(from_y, half, last_send.at[3, step], last_recv.at[3, step], other_x)
        six.start()
        mids[step] += [five, six]
    own[0].wait()
    for step in range(planes):
        for which in range(2, 6):
            mids[step][which].wait_recv()
        base = lax.rem(plane + planes - step, planes) * 4
        loads = [
            pltpu.make_async_copy(ga_ref.at[base + part], tiles.at[part], tile_sem.at[part])
            for part in range(4)
        ]
        for copy in loads:
            copy.start()
        for copy in loads:
            copy.wait()

        @pl.loop(0, 4)
        def _(part):
            at = pl.ds(pl.multiple_of((base + part) * rows, rows), rows)
            grad_ref[at, :] = lax.dot_general(
                tiles[part], w_ref[...], (((1,), (1,)), ((), ())), preferred_element_type=F32
            ).astype(BF16)

        for copy in mids[step]:
            copy.wait_send()
    for number, copy in enumerate(waits):
        if number >= planes - 1:
            copy.wait_recv()
        copy.wait_send()
    for copy in own[1:]:
        copy.wait()


def attend(local_heads, chosen_ref, q_ref, k_ref, v_ref, g_ref, o_ref, dq_ref, dk_ref, dv_ref,
           dk_acc, dv_acc):
    length = q_ref.shape[0]
    blocks = length // BLOCK
    scaling = DH ** (-0.5)
    dk_acc[...] = jnp.zeros_like(dk_acc)
    dv_acc[...] = jnp.zeros_like(dv_acc)

    def nt(a, b):
        return lax.dot_general(a, b, (((1,), (1,)), ((), ())), preferred_element_type=F32)

    def nn(a, b):
        return lax.dot_general(a, b, (((1,), (0,)), ((), ())), preferred_element_type=F32)

    def tn(a, b):
        return lax.dot_general(a, b, (((0,), (0,)), ((), ())), preferred_element_type=F32)

    def at(block):
        return pl.ds(pl.multiple_of(block * BLOCK, BLOCK), BLOCK)

    def stacked(ref, block):
        rows = ref[at(block), :]
        return jnp.concatenate([rows[:, h * DH:(h + 1) * DH] for h in range(local_heads)], axis=0)

    def unstack(ref, block, value):
        ref[at(block), :] = jnp.concatenate(
            [value[h * BLOCK:(h + 1) * BLOCK] for h in range(local_heads)], axis=1
        ).astype(BF16)

    q = stacked(q_ref, 0)
    g = stacked(g_ref, 0)
    s = nt(q, k_ref[...]) * scaling
    e = jnp.exp(s - jnp.max(s, axis=1, keepdims=True))
    p = e * (1.0 / jnp.sum(e, axis=1, keepdims=True))
    pb = p.astype(BF16)
    o = nn(pb, v_ref[...]).astype(BF16)
    unstack(o_ref, 0, o)
    row_dot = jnp.sum(g.astype(F32) * o.astype(F32), axis=1, keepdims=True)
    ds = (p * (nt(g, v_ref[...]) - row_dot)).astype(BF16)
    unstack(dq_ref, 0, nn(ds, k_ref[...]) * scaling)
    dk_acc[...] += tn(ds, q)
    dv_acc[...] += tn(pb, g)

    def body(i, carry):
        right = jnp.minimum(i + 1, blocks - 1)
        near = [0, i - 1, i, right]
        picked = [chosen_ref[h, i - 1] for h in range(local_heads)]
        q = stacked(q_ref, i)
        g = stacked(g_ref, i)
        kn = jnp.concatenate([k_ref[at(b), :] for b in near], axis=0)
        vn = jnp.concatenate([v_ref[at(b), :] for b in near], axis=0)
        kr = [k_ref[at(b), :] for b in picked]
        vr = [v_ref[at(b), :] for b in picked]

        def per_head(op, a, b):
            return jnp.concatenate(
                [op(a[h * BLOCK:(h + 1) * BLOCK], b[h]) for h in range(local_heads)], axis=0
            )

        sn = nt(q, kn) * scaling
        s1 = jnp.where(i >= 2, sn[:, BLOCK:2 * BLOCK], -jnp.inf)
        s3 = jnp.where(i <= blocks - 2, sn[:, 3 * BLOCK:], -jnp.inf)
        s = jnp.concatenate(
            [sn[:, :BLOCK], s1, sn[:, 2 * BLOCK:3 * BLOCK], s3, per_head(nt, q, kr) * scaling], axis=1
        )
        e = jnp.exp(s - jnp.max(s, axis=1, keepdims=True))
        p = e * (1.0 / jnp.sum(e, axis=1, keepdims=True))
        pb = p.astype(BF16)
        pn, pr = pb[:, :4 * BLOCK], pb[:, 4 * BLOCK:]
        o = (nn(pn, vn) + per_head(nn, pr, vr)).astype(BF16)
        unstack(o_ref, i, o)
        row_dot = jnp.sum(g.astype(F32) * o.astype(F32), axis=1, keepdims=True)
        dp = jnp.concatenate([nt(g, vn), per_head(nt, g, vr)], axis=1)
        ds = (p * (dp - row_dot)).astype(BF16)
        dn, dr = ds[:, :4 * BLOCK], ds[:, 4 * BLOCK:]
        unstack(dq_ref, i, (nn(dn, kn) + per_head(nn, dr, kr)) * scaling)
        dkn = tn(dn, q)
        dvn = tn(pn, g)
        for slot, b in enumerate(near):
            dk_acc[at(b), :] += dkn[slot * BLOCK:(slot + 1) * BLOCK]
            dv_acc[at(b), :] += dvn[slot * BLOCK:(slot + 1) * BLOCK]
        for h in range(local_heads):
            rows = slice(h * BLOCK, (h + 1) * BLOCK)
            dk_acc[at(picked[h]), :] += tn(dr[rows], q[rows])
            dv_acc[at(picked[h]), :] += tn(pr[rows], g[rows])
        return carry

    lax.fori_loop(1, blocks, body, 0)
    dk_ref[...] = (dk_acc[...] * scaling).astype(BF16)
    dv_ref[...] = dv_acc[...].astype(BF16)


def bring_back(n, m, kv_heads, o_ref, dq_ref, dk_ref, dv_ref, g_ref, oo_ref, dqo_ref, dko_ref, dvo_ref,
               dw_ref, k_parts, v_parts, own_half, theirs_half, both_half, w_own, w_parts, o_vmem, o_turned, g_vmem, own_sem, send, recv, w_send, w_recv):
    rows = oo_ref.shape[0]
    width = o_ref.shape[1]
    me = lax.axis_index("context")
    sequence = lax.axis_index("dp")
    greet(n, m)
    cols = pl.ds(pl.multiple_of(me * width, DH), width)
    pairs = (
        (o_ref, oo_ref.at[:, cols]),
        (dq_ref, dqo_ref.at[:, cols]),
    )
    copies = []

    def send_out(kinds):
        for step in range(1, n):
            device = lax.rem(me + step, n)
            theirs = pl.ds(pl.multiple_of(device * rows, rows), rows)
            for kind in kinds:
                src, dst = pairs[kind]
                copy = pltpu.make_async_remote_copy(
                    src_ref=src.at[theirs, :], dst_ref=dst, send_sem=send.at[kind, step],
                    recv_sem=recv.at[kind, step], device_id=(sequence, device), device_id_type=MESH,
                )
                copy.start()
                copies.append(copy)

    load_o = pltpu.make_async_copy(o_ref, o_vmem, own_sem.at[4])
    load_g = pltpu.make_async_copy(g_ref, g_vmem, own_sem.at[5])
    side = lax.rem(me, 2)
    pair = me // 2
    swaps = []
    for kind, ref in enumerate((dk_ref, dv_ref)):
        copy = pltpu.make_async_remote_copy(
            src_ref=ref.at[:, 1 - side], dst_ref=theirs_half.at[kind], send_sem=send.at[2 + kind, 0],
            recv_sem=recv.at[2 + kind, 0], device_id=(sequence, me + 1 - 2 * side), device_id_type=MESH,
        )
        copy.start()
        swaps.append(copy)
    halves = [
        pltpu.make_async_copy(ref.at[:, side], own_half.at[kind], own_sem.at[2 + kind])
        for kind, ref in enumerate((dk_ref, dv_ref))
    ]
    for copy in halves:
        copy.start()
    load_o.start()
    load_g.start()
    send_out((0,))
    mine = pl.ds(pl.multiple_of(me * rows, rows), rows)
    own = [
        pltpu.make_async_copy(src.at[mine, :], dst, own_sem.at[kind])
        for kind, (src, dst) in enumerate(pairs)
    ]
    load_o.wait()

    @pl.loop(0, n)
    def _(t):
        at = pl.ds(pl.multiple_of(t * rows, rows), rows)
        o_turned[:, at] = o_vmem[at, :].T

    load_g.wait()
    wide = 256

    @pl.loop(0, g_ref.shape[1] // wide)
    def _(t):
        at = pl.ds(pl.multiple_of(t * wide, wide), wide)
        w_own[:, at] = lax.dot_general(
            o_turned[...], g_vmem[:, at], (((1,), (0,)), ((), ())), preferred_element_type=F32
        ).astype(BF16)

    w_copies = []
    for step in range(1, m):
        copy = pltpu.make_async_remote_copy(
            src_ref=w_own, dst_ref=w_parts.at[sequence], send_sem=w_send.at[step],
            recv_sem=w_recv.at[step], device_id=(lax.rem(sequence + step, m), me), device_id_type=MESH,
        )
        copy.start()
        w_copies.append(copy)
    send_out((1,))
    for copy in swaps + halves:
        copy.wait()

    @pl.loop(0, n // 2)
    def _(t):
        for kind in range(2):
            both_half[kind, t] = (
                own_half[kind, t].astype(F32) + theirs_half[kind, t].astype(F32)
            ).astype(BF16)

    for step in range(1, n // 2):
        slot = lax.rem(pair + step, n // 2)
        for kind, parts in enumerate((k_parts, v_parts)):
            copy = pltpu.make_async_remote_copy(
                src_ref=both_half.at[kind, slot], dst_ref=parts.at[pair], send_sem=send.at[2 + kind, step],
                recv_sem=recv.at[2 + kind, step], device_id=(sequence, slot * 2 + side),
                device_id_type=MESH,
            )
            copy.start()
            copies.append(copy)
    for kind, parts in enumerate((k_parts, v_parts)):
        own.append(pltpu.make_async_copy(both_half.at[kind, pair], parts.at[pair], own_sem.at[2 + kind]))
    for copy in own:
        copy.start()
    to_slot = pltpu.make_async_copy(w_own, w_parts.at[sequence], own_sem.at[6])
    to_slot.start()
    to_slot.wait()
    for copy in w_copies:
        copy.wait()
    tile = 32

    @pl.loop(0, w_own.shape[0] // tile)
    def _(t):
        at = pl.ds(pl.multiple_of(t * tile, tile), tile)
        total = w_parts[0, at, :].astype(F32)
        for other in range(1, m):
            total = total + w_parts[other, at, :].astype(F32)
        dw_ref[at, :] = total

    for copy in own:
        copy.wait()
    for copy in copies:
        copy.wait()
    per = n // 2 // kv_heads
    for parts, out in ((k_parts, dko_ref), (v_parts, dvo_ref)):
        for kv in range(kv_heads):
            total = parts[kv * per].astype(F32)
            for other in range(1, per):
                total = total + parts[kv * per + other].astype(F32)
            out[:, kv * DH:(kv + 1) * DH] = total.astype(BF16)


def local(queries, keys, values, d_proj, out_weight, random_blocks):
    n = lax.axis_size("context")
    m = lax.axis_size("dp")
    rows = queries.shape[1]
    heads = queries.shape[2] // DH
    kv_heads = keys.shape[2] // DH
    group = heads // kv_heads
    local_heads = heads // n
    width = local_heads * DH
    columns = d_proj.shape[2]
    length = rows * n
    planes = n // 4
    anywhere = pl.BlockSpec(memory_space=pl.ANY)
    vmem = pl.BlockSpec(memory_space=pltpu.VMEM)
    shape = jax.ShapeDtypeStruct
    dma = pltpu.SemaphoreType.DMA

    q_all, k_all, v_all, g_all, grad_out = pl.pallas_call(
        functools.partial(spread, n, local_heads, group),
        out_shape=(
            shape((length, width), BF16),
            shape((length, DH), BF16),
            shape((length, DH), BF16),
            shape((n, rows, columns), BF16),
            shape((length, width), BF16),
        ),
        in_specs=[anywhere] * 4 + [vmem],
        out_specs=(anywhere,) * 4 + (vmem,),
        scratch_shapes=[
            pltpu.VMEM((4, rows, columns), BF16),
            dma((4,)),
            dma((4,)),
            dma((3, n)), dma((3, n)),
            dma((planes,)), dma((planes,)),
            dma((2, planes)), dma((2, planes)),
            dma((4, planes)), dma((4, planes)),
        ],
        compiler_params=pltpu.CompilerParams(
            collective_id=0, has_side_effects=True, vmem_limit_bytes=56 * 1024 * 1024
        ),
        name="spread",
    )(queries[0], keys[0], values[0], d_proj[0], out_weight)

    chosen = lax.dynamic_slice_in_dim(
        random_blocks, lax.axis_index("context") * local_heads, local_heads, 0
    )
    out, dq, dk, dv = pl.pallas_call(
        functools.partial(attend, local_heads),
        out_shape=(
            shape((length, width), BF16),
            shape((length, width), BF16),
            shape((length, DH), BF16),
            shape((length, DH), BF16),
        ),
        in_specs=[pl.BlockSpec(memory_space=pltpu.SMEM)] + [vmem] * 4,
        out_specs=(vmem,) * 4,
        scratch_shapes=[pltpu.VMEM((length, DH), F32), pltpu.VMEM((length, DH), F32)],
        compiler_params=pltpu.CompilerParams(vmem_limit_bytes=48 * 1024 * 1024),
        name="attend",
    )(chosen, q_all, k_all, v_all, grad_out)
    attended, d_queries, d_keys, d_values, d_weight = pl.pallas_call(
        functools.partial(bring_back, n, m, kv_heads),
        out_shape=(
            shape((rows, heads * DH), BF16),
            shape((rows, heads * DH), BF16),
            shape((rows, kv_heads * DH), BF16),
            shape((rows, kv_heads * DH), BF16),
            shape((width, columns), F32),
        ),
        in_specs=[anywhere] * 5,
        out_specs=(anywhere, anywhere, vmem, vmem, vmem),
        scratch_shapes=[
            pltpu.VMEM((n // 2, rows, DH), BF16),
            pltpu.VMEM((n // 2, rows, DH), BF16),
            pltpu.VMEM((2, n // 2, rows, DH), BF16),
            pltpu.VMEM((2, n // 2, rows, DH), BF16),
            pltpu.VMEM((2, n // 2, rows, DH), BF16),
            pltpu.VMEM((width, columns), BF16),
            pltpu.VMEM((m, width, columns), BF16),
            pltpu.VMEM((length, width), BF16),
            pltpu.VMEM((width, length), BF16),
            pltpu.VMEM((length, columns), BF16),
            dma((7,)),
            dma((4, n)), dma((4, n)),
            dma((m,)), dma((m,)),
        ],
        compiler_params=pltpu.CompilerParams(
            collective_id=1, has_side_effects=True, vmem_limit_bytes=48 * 1024 * 1024
        ),
        name="bring_back",
    )(out, dq, dk.reshape(n // 2, 2, rows, DH), dv.reshape(n // 2, 2, rows, DH), g_all.reshape(length, columns))
    return (attended[None], d_queries[None], d_keys[None], d_values[None], d_weight)


def solution(mesh):
    in_specs = (
        P("dp", "context", None),
        P("dp", "context", None),
        P("dp", "context", None),
        P("dp", "context", None),
        P("context", None),
        P(),
    )
    out_specs = (
        P("dp", "context", None),
        P("dp", "context", None),
        P("dp", "context", None),
        P("dp", "context", None),
        P("context", None),
    )
    return jax.shard_map(local, mesh=mesh, in_specs=in_specs, out_specs=out_specs, check_vma=False)
```
